32 devices in a mesh: member: 2 (over y), row: 4 (over z), col: 2 (over x), sub: 2 (over core).
Axes of the slice: x: 2, y: 2, z: 4, core: 2. Of those that a mesh axis runs over, the one named last changes fastest.
Arguments:
- kernel: float32 [12288, 12288], P('row', ('col', 'sub')), may hold values from -0.0546875 to 0.0546875
- log_rate: float32 [512, 12288], P(('member', 'col', 'sub'), 'row'), parts along dimension 0, may hold values from -1 to 1
- state: float32 [512, 12288], P(('member', 'col', 'sub'), 'row'), parts along dimension 0, may hold values from -1 to 1
- base_stress: float32 [512, 12288], P(('member', 'col', 'sub'), 'row'), parts along dimension 0, may hold values from 1 to 4
- friction: float32 [12288], P('row'), may hold values from 0.5 to 2
- region: int32 [12288], P('row'), may hold values 0 or 1
- adjacency: int32 [12288], P('row'), may hold values from 0 to 12287, as said below
Outputs:
- final_rate: float32 [512, 12288], P(('member', 'col', 'sub'), 'row'), parts along dimension 0
- stress: float32 [512, 12288], P(('member', 'col', 'sub'), 'row'), parts along dimension 0
The draws below stay inside these ranges and needn't reach their ends.
There are 2 independent parts, one for each index of `member`. The reference program is written for one: setup_inputs(seed, part) draws one part's arguments, and reference() takes and returns one part's arrays. A program takes and returns all parts, laid end to end along the dimension named above; an argument that names none is the same for every part. Nothing has to cross between parts.
Inputs may be any that keep to these rules, and one draw needn't show every extreme that they name: `region`: 1 marks a volume cell, 0 a fault patch. `adjacency`: each unknown's partner lies in the same aligned block of 3072 unknowns.
All inputs are finite; a program needn't handle non-finite values. No bound on the sum of `region` on one device may be relied on, other than what follows from the above.
Results may differ from the reference program's by a relative error of at most 0.0003.
Values sent between devices are 32-bit elements; how exact they have to be, the bound alone decides.
No kernel may reach another device: no remote copies, remote signals or barrier semaphores. Data moves between devices by JAX's collectives and lax.ppermute only.
A program may use at most 128 MiB of HBM per device.

```python
import math
import jax
import jax.numpy as jnp
from jax import lax

NU = 12288
SAMPLES = 256
NEWTON = 4
ROWB = 3072


def draw_adjacency(key, part):
    blocks = jnp.arange(NU, dtype=jnp.int32) // ROWB * ROWB
    offset = jax.random.randint(jax.random.fold_in(key, 17), (NU,), 0, ROWB, dtype=jnp.int32)
    return (blocks + offset).astype(jnp.int32)


def place_ends(drawn, stream_key, smallest, high):
    longest = drawn.shape.index(max(drawn.shape))
    spots = []
    for shift in (0, 1):
        where = [jax.random.randint(jax.random.fold_in(stream_key, axis), (), 0, length) for axis, length in enumerate(drawn.shape)]
        where[longest] = (where[longest] + shift) % drawn.shape[longest]
        spots.append(tuple(where))
    return drawn.at[spots[0]].set(smallest).at[spots[1]].set(high)


def level_of(stream_key, shape, cuts, least, high):
    def one(position, blocks):
        heights = jax.random.uniform(jax.random.fold_in(jax.random.fold_in(stream_key, 6), position), (blocks,), jnp.float32, least / len(cuts), high / len(cuts))
        return jnp.repeat(jnp.exp(heights), shape[position] // blocks).reshape((-1,) + (1,) * (len(shape) - position - 1))

    loudness = one(*cuts[0])
    for cut in cuts[1:]:
        loudness = loudness * one(*cut)
    return loudness


def scatter_about(stream_key, extent, deviation, limit, split=(), kind=jnp.bfloat16):
    result = deviation * jax.random.normal(stream_key, extent, jnp.float32)
    if split:
        result = result * level_of(stream_key, extent, split, -0.22, 0.18)
    return jnp.clip(result, -limit, limit).astype(kind)


def setup_inputs(seed: int = 0, part: int = 0) -> dict:
    keys = jax.random.split(jax.random.key(seed), 8)
    part_splits = jax.random.split(jax.random.fold_in(keys[7], part), 8)
    kernel = scatter_about(keys[0], (NU, NU), NU ** -0.5, 0.0546875, ((0, 4), (1, 4)), jnp.float32)
    log_rate = jnp.clip(jax.random.uniform(part_splits[1], (SAMPLES, NU), jnp.float32, -1.0, 1.0) * level_of(part_splits[1], (SAMPLES, NU), ((0, 4), (1, 4)), -0.4, 0.0), -1.0, 1.0)
    state = jnp.clip(jax.random.uniform(part_splits[2], (SAMPLES, NU), jnp.float32, -1.0, 1.0) * level_of(part_splits[2], (SAMPLES, NU), ((0, 4), (1, 4)), -0.4, 0.0), -1.0, 1.0)
    base_stress = jnp.clip(1.0 + 3.0 * jax.random.uniform(part_splits[3], (SAMPLES, NU), jnp.float32) ** level_of(part_splits[3], (SAMPLES, NU), ((0, 4), (1, 4)), -0.2, 0.2), 1.0, 4.0)
    friction = jnp.clip(jnp.exp(math.log(2.0) - 1.3862944 * jax.random.uniform(keys[4], (NU,), jnp.float32) ** level_of(keys[4], (NU,), ((0, 4),), -0.2, 0.2)), 0.5, 2.0)
    region = place_ends((jax.random.randint(keys[5], (NU,), 0, 3) < 1).astype(jnp.int32), jax.random.fold_in(keys[5], 1), 0, 1)
    adjacency = draw_adjacency(jax.random.fold_in(keys[7], 71), part)
    return dict(kernel=kernel, log_rate=log_rate, state=state, base_stress=base_stress, friction=friction, region=region, adjacency=adjacency)


coupling = 0.3
step_size = 0.5

def couple(stress, adjacency):
    return stress + coupling * (jnp.take(stress, adjacency, axis=1) - stress)

def solve(log_rate, state, stress, friction, volume):
    value = log_rate
    for turn in range(NEWTON):
        expo = jnp.exp(value)
        slipx = jnp.exp(value + state)
        root = jnp.sqrt(1.0 + slipx * slipx)
        fault_f = friction * jnp.log(slipx + root)
        fault_d = friction * slipx / root
        creep = jnp.exp(state + value / 3.0)
        cell_f = friction * creep
        cell_d = friction * creep / 3.0
        resid = jnp.where(volume, cell_f, fault_f) + expo - stress
        deriv = jnp.where(volume, cell_d, fault_d) + expo
        value = value - jnp.clip(resid / deriv, -1.0, 1.0)
    return value

def rates_times(rates, kernel):
    return lax.dot_general(rates, kernel, (((1,), (1,)), ((), ())), precision=lax.Precision.HIGHEST, preferred_element_type=jnp.float32)

def reference(kernel, log_rate, state, base_stress, friction, region, adjacency):
    volume = (region == 1)[None, :]
    fric = friction[None, :]
    first = rates_times(jnp.exp(log_rate), kernel)
    section_one = solve(log_rate, state, couple(base_stress + step_size * first, adjacency), fric, volume)
    second = rates_times(jnp.exp(section_one), kernel)
    stress = couple(base_stress + 0.5 * step_size * (first + second), adjacency)
    final_rate = solve(section_one, state, stress, fric, volume)
    return (final_rate, stress)
```

```python
import jax
import jax.numpy as jnp
from jax import lax
from jax.experimental import pallas as pl
from jax.experimental.pallas import tpu as pltpu
from jax.sharding import PartitionSpec as P

NEWTON = 4
CHUNKS = 2
LANES = 128
SLOTS = 4

coupling = 0.3
step_size = 0.5

f32 = jnp.float32
bf16 = jnp.bfloat16
NT = (((1,), (1,)), ((), ()))
VMEM = pl.BlockSpec(memory_space=pltpu.VMEM)
ANY = pl.BlockSpec(memory_space=pl.ANY)


def newton(value, state, stress, friction, volume):
    grow = jnp.exp(state)
    for turn in range(NEWTON):
        expo = jnp.exp(value)
        slipx = expo * grow
        square = 1.0 + slipx * slipx
        inverse = lax.rsqrt(square)
        fault_f = jnp.log(slipx + square * inverse)
        fault_d = slipx * inverse
        creep = grow * jnp.exp(value * (1.0 / 3.0))
        part_f = friction * jnp.where(volume, creep, fault_f)
        part_d = friction * jnp.where(volume, creep * (1.0 / 3.0), fault_d)
        value = value - jnp.clip((part_f + expo - stress) / (part_d + expo), -1.0, 1.0)
    return value


def step_kernel(scale, n_sum, last, base, value, state, sums, friction, region, partner):
    high, wide = base.shape
    tiles = wide // LANES

    def body(*refs):
        base_ref, value_ref, state_ref = refs[:3]
        sum_refs = refs[3 : 3 + n_sum]
        friction_ref, region_ref, partner_ref = refs[3 + n_sum : 6 + n_sum]
        outs = refs[6 + n_sum : -1]
        raw = refs[-1]
        total = sum_refs[0][...]
        for ref in sum_refs[1:]:
            total = total + ref[...]
        if not last:
            outs[2][...] = total
        raw[...] = base_ref[...] + scale * total

        def tile(j, _):
            cols = pl.ds(pl.multiple_of(j * LANES, LANES), LANES)
            where = jnp.broadcast_to(partner_ref[:, cols], (8, LANES))
            lane = where % LANES
            block = where // LANES
            groups = high // 8
            moved = [jnp.zeros((8, LANES), f32) for _ in range(groups)]
            for k in range(tiles):
                here = block == k
                for g in range(groups):
                    got = jnp.take_along_axis(
                        raw[pl.ds(g * 8, 8), pl.ds(k * LANES, LANES)], lane, axis=1, mode="promise_in_bounds"
                    )
                    moved[g] = jnp.where(here, got, moved[g])
            fric = jnp.broadcast_to(friction_ref[:, cols], (8, LANES))
            volume = jnp.broadcast_to(region_ref[:, cols], (8, LANES)) == 1
            for g in range(groups):
                rows = pl.ds(g * 8, 8)
                own = raw[rows, cols]
                stress = own + coupling * (moved[g] - own)
                new = newton(value_ref[rows, cols], state_ref[rows, cols], stress, fric, volume)
                outs[0][rows, cols] = new
                outs[1][rows, cols] = stress if last else jnp.exp(new)
            return 0

        lax.fori_loop(0, tiles, tile, 0)

    return pl.pallas_call(
        body,
        in_specs=[VMEM] * (6 + n_sum),
        out_specs=[VMEM] * (2 if last else 3),
        out_shape=[jax.ShapeDtypeStruct((high, wide), f32)] * (2 if last else 3),
        scratch_shapes=[pltpu.VMEM((high, wide), f32)],
        compiler_params=pltpu.CompilerParams(vmem_limit_bytes=24 << 20),
        cost_estimate=pl.CostEstimate(flops=200 * high * wide, bytes_accessed=28 * high * wide, transcendentals=20 * high * wide),
    )(base, value, state, *sums, friction, region, partner)


def rates_times(pieces, kernel, tile=128):
    count = len(pieces)
    high, depth = pieces[0].shape
    rows = kernel.shape[0]
    much = count * high
    steps = rows // tile
    slots = min(SLOTS, steps)

    def body(*refs):
        parts, kernel_ref, outs = refs[:count], refs[count], refs[count + 1 : 2 * count + 1]
        stacked, held, sem = refs[2 * count + 1 :]

        def fetch(i, slot):
            return pltpu.make_async_copy(
                kernel_ref.at[pl.ds(pl.multiple_of(i * tile, tile), tile), :], held.at[slot], sem.at[slot]
            )

        for i in range(slots - 1):
            fetch(i, i).start()
        for p in range(count):
            whole = parts[p][...]
            upper = whole.astype(bf16)
            stacked[pl.ds(p * high, high), :] = upper
            stacked[pl.ds(much + p * high, high), :] = (whole - upper.astype(f32)).astype(bf16)

        def step(i, _):
            slot = lax.rem(i, slots)

            @pl.when(i + slots - 1 < steps)
            def _():
                fetch(i + slots - 1, lax.rem(i + slots - 1, slots)).start()

            fetch(i, slot).wait()
            whole = held[slot]
            upper = whole.astype(bf16)
            lower = (whole - upper.astype(f32)).astype(bf16)
            both = lax.dot_general(stacked[...], upper, NT, preferred_element_type=f32)
            rest = lax.dot_general(stacked[pl.ds(0, much), :], lower, NT, preferred_element_type=f32)
            total = both[:much] + both[much:] + rest
            cols = pl.ds(pl.multiple_of(i * tile, tile), tile)
            for p in range(count):
                outs[p][:, cols] = total[p * high : (p + 1) * high]
            return 0

        lax.fori_loop(0, steps, step, 0)

    return pl.pallas_call(
        body,
        in_specs=[VMEM] * count + [ANY],
        out_specs=[VMEM] * count,
        out_shape=[jax.ShapeDtypeStruct((high, rows), f32)] * count,
        scratch_shapes=[
            pltpu.VMEM((2 * much, depth), bf16),
            pltpu.VMEM((slots, tile, depth), f32),
            pltpu.SemaphoreType.DMA((slots,)),
        ],
        compiler_params=pltpu.CompilerParams(vmem_limit_bytes=32 << 20),
        cost_estimate=pl.CostEstimate(
            flops=6 * much * rows * depth, bytes_accessed=4 * rows * depth, transcendentals=0
        ),
    )(*pieces, kernel)


def spread_small(rates):
    row = lax.axis_index("row")
    here = lax.axis_index(("col", "sub"))
    up1 = lax.ppermute(rates, "row", [(0, 1), (1, 2), (2, 3)])
    down1 = lax.ppermute(rates, "row", [(1, 0), (2, 1), (3, 2)])
    up2 = lax.ppermute(up1, "row", [(1, 2), (2, 3)])
    down2 = lax.ppermute(down1, "row", [(1, 0), (2, 1)])
    far = lax.ppermute(jnp.where(row == 1, up1, down1), "row", [(1, 3), (2, 0)])
    near2 = jnp.where(row >= 2, up2, down2)
    pieces = []
    for flip in range(4):
        away = (here ^ flip) - row
        picked = jnp.where(
            away == 0,
            rates,
            jnp.where(
                away == 1,
                down1,
                jnp.where(away == -1, up1, jnp.where(jnp.abs(away) == 2, near2, far)),
            ),
        )
        if flip:
            picked = lax.ppermute(picked, ("col", "sub"), [(i, i ^ flip) for i in range(4)])
        pieces.append(picked)
    return pieces


def total_small(parts):
    other = [(i, i ^ 1) for i in range(4)]
    across = [(i, i ^ 2) for i in range(4)]
    mine = lax.ppermute(parts[1], ("col", "sub"), other)
    theirs = parts[2] + lax.ppermute(parts[3], ("col", "sub"), other)
    return [parts[0], mine, lax.ppermute(theirs, ("col", "sub"), across)]


def spread_any(rates):
    blocks = lax.all_gather(rates, "row", axis=0)
    pieces = lax.all_to_all(blocks, ("col", "sub"), 0, 0)
    return [pieces[p] for p in range(pieces.shape[0])]


def total_any(parts):
    return [lax.psum_scatter(jnp.concatenate(parts, axis=0), ("col", "sub"), scatter_dimension=0, tiled=True)]


def solution(mesh):
    small = mesh.shape["row"] == 4 and mesh.shape["col"] == 2 and mesh.shape["sub"] == 2
    spread, total = (spread_small, total_small) if small else (spread_any, total_any)

    def per_device(kernel, log_rate, state, base_stress, friction, region, adjacency):
        rows = kernel.shape[0]
        samples = log_rate.shape[0]
        partner = (adjacency - lax.axis_index("row") * rows)[None, :]
        region = region[None, :]
        friction = friction[None, :]
        chunks = CHUNKS if small else 1
        high = samples // chunks
        cut = [slice(k * high, (k + 1) * high) for k in range(chunks)]

        pieces = [spread(jnp.exp(log_rate[s])) for s in cut]
        middle = []
        for k, s in enumerate(cut):
            sums = total(rates_times(pieces[k], kernel))
            value, rates, first = step_kernel(
                step_size, len(sums), False, base_stress[s], log_rate[s], state[s], sums, friction, region, partner
            )
            middle.append((value, first, spread(rates)))
        done = []
        for k, s in enumerate(cut):
            value, first, pieces = middle[k]
            sums = [first] + total(rates_times(pieces, kernel))
            done.append(
                step_kernel(
                    0.5 * step_size, len(sums), True, base_stress[s], value, state[s], sums, friction, region, partner
                )
            )
        return (
            jnp.concatenate([d[0] for d in done], axis=0),
            jnp.concatenate([d[1] for d in done], axis=0),
        )

    in_specs = (
        P("row", ("col", "sub")),
        P(("member", "col", "sub"), "row"),
        P(("member", "col", "sub"), "row"),
        P(("member", "col", "sub"), "row"),
        P("row"),
        P("row"),
        P("row"),
    )
    out_specs = (P(("member", "col", "sub"), "row"), P(("member", "col", "sub"), "row"))
    return jax.shard_map(per_device, mesh=mesh, in_specs=in_specs, out_specs=out_specs, check_vma=False)
```

```python
import jax
import jax.numpy as jnp
from jax import lax
from jax.experimental import pallas as pl
from jax.experimental.pallas import tpu as pltpu
from jax.sharding import PartitionSpec as P

NEWTON = 4
LANES = 128
PARTS = 2

coupling = 0.3
step_size = 0.5

f32 = jnp.float32
bf16 = jnp.bfloat16
NT = (((1,), (1,)), ((), ()))
CORNER = pl.BlockSpec((8, LANES), lambda *_: (0, 0))


def newton(value, state, stress, friction, volume):
    grow = jnp.exp(state)
    for turn in range(NEWTON):
        expo = jnp.exp(value)
        slipx = expo * grow
        square = 1.0 + slipx * slipx
        inverse = lax.rsqrt(square)
        fault_f = jnp.log(slipx + square * inverse)
        fault_d = slipx * inverse
        creep = grow * jnp.exp(value * (1.0 / 3.0))
        part_f = friction * jnp.where(volume, creep, fault_f)
        part_d = friction * jnp.where(volume, creep * (1.0 / 3.0), fault_d)
        value = value - jnp.clip((part_f + expo - stress) / (part_d + expo), -1.0, 1.0)
    return value


def step_kernel(scale, last, part, parts, base, value, state, sums, first, friction, region, partner):
    high, wide = base.shape
    tiles = wide // LANES
    terms = [a for group in sums for a in group] + ([first] if last else [])
    n_sum = len(terms)
    n_value = len(value)
    span = wide // parts
    width = wide // len(sums)
    each = len(sums[0])

    def body(*refs):
        base_ref, state_ref, value_refs = refs[0], refs[1], refs[2 : 2 + n_value]
        sum_refs = refs[2 + n_value : 2 + n_value + n_sum]
        friction_ref, region_ref, partner_ref = refs[2 + n_value + n_sum : 5 + n_value + n_sum]
        outs = refs[5 + n_value + n_sum : -1]
        raw = refs[-1]
        for k in range(len(sums)):
            cols = pl.ds(k * width, width)
            total = sum_refs[k * each][...]
            for ref in sum_refs[k * each + 1 : (k + 1) * each]:
                total = total + ref[pl.ds(0, high), :]
            if last:
                total = sum_refs[-1][:, cols] + total
            elif part == 0:
                outs[2][:, cols] = total
            raw[:, cols] = base_ref[:, cols] + scale * total

        def tiles_of(value_ref, begin, count):
            def tile(j, _):
                there = pl.ds(pl.multiple_of(j * LANES, LANES), LANES)
                cols = pl.ds(pl.multiple_of(part * span + begin + j * LANES, LANES), LANES)
                into = pl.ds(pl.multiple_of(begin + j * LANES, LANES), LANES)
                where = jnp.broadcast_to(partner_ref[:, cols], (8, LANES))
                lane = where % LANES
                block = where // LANES
                groups = high // 8
                moved = [jnp.zeros((8, LANES), f32) for _ in range(groups)]
                for k in range(tiles):
                    here = block == k
                    for g in range(groups):
                        got = jnp.take_along_axis(
                            raw[pl.ds(g * 8, 8), pl.ds(k * LANES, LANES)], lane, axis=1, mode="promise_in_bounds"
                        )
                        moved[g] = jnp.where(here, got, moved[g])
                fric = jnp.broadcast_to(friction_ref[:, cols], (8, LANES))
                volume = jnp.broadcast_to(region_ref[:, cols], (8, LANES)) == 1
                for g in range(groups):
                    rows = pl.ds(g * 8, 8)
                    own = raw[rows, cols]
                    stress = own + coupling * (moved[g] - own)
                    new = newton(value_ref[rows, there], state_ref[rows, cols], stress, fric, volume)
                    outs[0][rows, into] = new
                    outs[1][rows, into] = stress if last else jnp.exp(new)
                return 0

            lax.fori_loop(0, count // LANES, tile, 0)

        for k in range(n_value):
            tiles_of(value_refs[k], k * (span // n_value), span // n_value)

    full = jax.ShapeDtypeStruct((high, wide), f32)
    some = jax.ShapeDtypeStruct((high, span), f32)
    out_shape = [some, some] + ([full] if part == 0 and not last else [])
    return pl.pallas_call(
        body,
        grid=(1,),
        in_specs=[whole(a.shape) for a in (base, state, *value, *terms, friction, region, partner)],
        out_specs=[whole(a.shape) for a in out_shape],
        out_shape=out_shape,
        scratch_shapes=[pltpu.VMEM((high, wide), f32)],
        compiler_params=pltpu.CompilerParams(vmem_limit_bytes=24 << 20),
        cost_estimate=pl.CostEstimate(flops=200 * high * span, bytes_accessed=28 * high * wide, transcendentals=20 * high * span),
    )(base, state, *value, *terms, friction, region, partner)


def whole(shape):
    return pl.BlockSpec(shape, lambda *_: (0, 0), pipeline_mode=pl.Buffered(1))


def rates_times(halves, choice, kernel, part, parts, deps, tile=256):
    high, depth = halves[0][0][0].shape
    much = 4 * high
    rows = kernel.shape[0] // parts
    tile = min(tile, rows)
    steps = rows // tile
    flat = [
        pltpu.with_memory_space_constraint(ref, pltpu.HBM) for pairs in halves for pair in pairs for ref in pair
    ]

    def body(choice_ref, *refs):
        ins, kernel_ref = refs[:16], refs[16]
        own, across, other, stacked, landed, sem = refs[17 + len(deps) :]

        @pl.when(pl.program_id(0) == 0)
        def _():
            def fetch(k, ref):
                return pltpu.make_async_copy(ref, landed.at[k], sem.at[k])

            for k in range(8):

                @pl.when(choice_ref[0] == 0)
                def _():
                    fetch(k, ins[2 * k]).start()

                @pl.when(choice_ref[0] != 0)
                def _():
                    fetch(k, ins[2 * k + 1]).start()

            for k in range(8):
                fetch(k, ins[2 * k]).wait()
                cols = pl.ds((k // 4) * depth, depth)
                row = (k % 4) * high
                rates = landed[k]
                rough = rates.astype(bf16)
                stacked[pl.ds(row, high), cols] = rough
                stacked[pl.ds(much + row, high), cols] = (rates - rough.astype(f32)).astype(bf16)

        block = kernel_ref[...]
        upper = block.astype(bf16)
        lower = (block - upper.astype(f32)).astype(bf16)
        both = lax.dot_general(stacked[...], upper, NT, preferred_element_type=f32)
        rest = lax.dot_general(stacked[pl.ds(0, much), :], lower, NT, preferred_element_type=f32)
        total = both[:much] + both[much:] + rest
        own[...] = total[:high]
        across[...] = total[2 * high : 3 * high]
        other[pl.ds(0, high), :] = total[high : 2 * high]
        other[pl.ds(high, high), :] = total[3 * high :]

    one = pl.BlockSpec((high, tile), lambda i: (0, i))
    two = pl.BlockSpec((2 * high, tile), lambda i: (0, i))
    return pl.pallas_call(
        body,
        grid=(steps,),
        in_specs=[pl.BlockSpec(memory_space=pltpu.SMEM)]
        + [pl.BlockSpec(memory_space=pltpu.HBM)] * 16
        + [pl.BlockSpec((tile, 2 * depth), lambda i: (part * steps + i, 0))]
        + [CORNER] * len(deps),
        out_specs=[one, one, two],
        out_shape=[
            jax.ShapeDtypeStruct((high, rows), f32),
            jax.ShapeDtypeStruct((high, rows), f32),
            jax.ShapeDtypeStruct((2 * high, rows), f32),
        ],
        scratch_shapes=[
            pltpu.VMEM((2 * much, 2 * depth), bf16),
            pltpu.VMEM((8, high, depth), f32),
            pltpu.SemaphoreType.DMA((8,)),
        ],
        compiler_params=pltpu.CompilerParams(vmem_limit_bytes=24 << 20),
        cost_estimate=pl.CostEstimate(
            flops=24 * much * rows * depth, bytes_accessed=8 * rows * depth, transcendentals=0
        ),
    )(choice, *flat, pltpu.with_memory_space_constraint(kernel, pltpu.HBM), *deps)


OUTER = [(0, 1), (1, 0), (2, 3), (3, 2)]
INNER = [(0, 0), (1, 2), (2, 1), (3, 3)]
PLANE = ("col", "sub")
CORE = [(i, i ^ 1) for i in range(4)]
ACROSS = [(i, i ^ 2) for i in range(4)]


def where_sent():
    row = lax.axis_index("row")
    return (row == 1) | (row == 2), lax.axis_index("col") == row // 2


def spread_one(rates):
    return [lax.ppermute(rates, "row", OUTER), lax.ppermute(rates, "row", INNER)]


def spread_two(near):
    return [lax.ppermute(near[1], "row", OUTER), lax.ppermute(near[0], "row", INNER)]


def spread_three(two):
    return lax.ppermute(two[1], "row", OUTER)


def shift(first, second):
    beside = where_sent()[1]
    mine = jnp.where(beside, first, second)
    sent = jnp.where(beside, second, first)
    got = lax.ppermute(sent, PLANE, ACROSS)
    return [mine, lax.ppermute(mine, PLANE, CORE), got, lax.ppermute(got, PLANE, CORE)]


def spread(rates):
    middle = where_sent()[0]
    near = spread_one(rates)
    two = spread_two(near)
    far = spread_three(two)
    one = shift(rates, jnp.where(middle, near[1], two[0]))
    return list(zip(one, shift(near[0], jnp.where(middle, two[1], far))))


def first_block():
    row = lax.axis_index("row")
    beside = lax.axis_index("col") == row // 2
    near = jnp.where(beside, row, jnp.where(row < 2, 2, 1))
    return (near % 2 != lax.axis_index("sub")).astype(jnp.int32)[None]


def once(array, guard):
    return jnp.where(guard == guard, array, 0.0)


def spread_any(rates):
    blocks = lax.all_gather(rates, "row", axis=0)
    pieces = lax.all_to_all(blocks, ("col", "sub"), 0, 0)
    return [pieces[p] for p in range(pieces.shape[0])]


def sums_any(pieces, kernel):
    rates = jnp.concatenate(pieces, axis=0)
    partial = lax.dot_general(rates, kernel, NT, precision=lax.Precision.HIGH, preferred_element_type=f32)
    return [[lax.psum_scatter(partial, ("col", "sub"), scatter_dimension=0, tiled=True)]]


def solution(mesh):
    small = mesh.shape["row"] == 4 and mesh.shape["col"] == 2 and mesh.shape["sub"] == 2

    def plain(kernel, log_rate, state, base_stress, labels):
        sums = sums_any(spread_any(jnp.exp(log_rate)), kernel)
        value, rates, first = step_kernel(step_size, False, 0, 1, base_stress, [log_rate], state, sums, None, *labels)
        sums = sums_any(spread_any(rates), kernel)
        return tuple(step_kernel(0.5 * step_size, True, 0, 1, base_stress, [value], state, sums, first, *labels))

    def chunked(kernel, log_rate, state, base_stress, labels):
        wide = kernel.shape[1]
        choice = first_block()
        cuts = [slice(k * wide // 2, (k + 1) * wide // 2) for k in range(2)]

        def product(halves):
            sums = []
            for part in range(PARTS):
                deps = [sums[0][0], before] if sums else []
                own, across, other = rates_times(halves, choice, kernel, part, PARTS, deps)
                if sums:
                    stacked = other.reshape(2, *own.shape)
                    other = once(stacked, sums[0][2][None]).reshape(other.shape)
                swapped = lax.ppermute(other, PLANE, CORE)
                before = across + swapped[own.shape[0] :]
                sums.append([own, swapped, lax.ppermute(before, PLANE, ACROSS)])
            return sums

        rates = jnp.exp(log_rate)
        ready = spread(rates[:, cuts[0]])
        sums = product([ready, spread(rates[:, cuts[1]])])
        value, rates, first = step_kernel(
            step_size, False, 0, 2, base_stress, [log_rate[:, cuts[0]]], state, sums, None, *labels
        )
        ready = spread(rates)
        other_value, rates = step_kernel(
            step_size, False, 1, 2, base_stress, [log_rate[:, cuts[1]]], state, sums, None, *labels
        )
        sums = product([ready, spread(rates)])
        return tuple(
            step_kernel(
                0.5 * step_size, True, 0, 1, base_stress, [value, other_value], state, sums, first, *labels
            )
        )

    def per_device(kernel, log_rate, state, base_stress, friction, region, adjacency):
        partner = (adjacency - lax.axis_index("row") * kernel.shape[0])[None, :]
        labels = (friction[None, :], region[None, :], partner)
        return (chunked if small else plain)(kernel, log_rate, state, base_stress, labels)

    in_specs = (
        P("row", ("col", "sub")),
        P(("member", "col", "sub"), "row"),
        P(("member", "col", "sub"), "row"),
        P(("member", "col", "sub"), "row"),
        P("row"),
        P("row"),
        P("row"),
    )
    out_specs = (P(("member", "col", "sub"), "row"), P(("member", "col", "sub"), "row"))
    return jax.shard_map(per_device, mesh=mesh, in_specs=in_specs, out_specs=out_specs, check_vma=False)
```

```python
import jax
import jax.numpy as jnp
from jax import lax
from jax.experimental import pallas as pl
from jax.experimental.pallas import tpu as pltpu
from jax.sharding import PartitionSpec as P

NEWTON = 4
LANES = 128
PARTS = 2

coupling = 0.3
step_size = 0.5

f32 = jnp.float32
bf16 = jnp.bfloat16
NT = (((1,), (1,)), ((), ()))
CORNER = pl.BlockSpec((8, LANES), lambda *_: (0, 0))


def newton(value, state, stress, friction, volume):
    grow = jnp.exp(state)
    for turn in range(NEWTON):
        expo = jnp.exp(value)
        slipx = expo * grow
        square = 1.0 + slipx * slipx
        inverse = lax.rsqrt(square)
        fault_f = jnp.log(slipx + square * inverse)
        fault_d = slipx * inverse
        creep = grow * jnp.exp(value * (1.0 / 3.0))
        part_f = friction * jnp.where(volume, creep, fault_f)
        part_d = friction * jnp.where(volume, creep * (1.0 / 3.0), fault_d)
        value = value - jnp.clip((part_f + expo - stress) / (part_d + expo), -1.0, 1.0)
    return value


def step_kernel(scale, last, part, parts, base, value, state, sums, first, friction, region, partner):
    high, wide = base.shape
    tiles = wide // LANES
    terms = [a for group in sums for a in group] + ([first] if last else [])
    n_sum = len(terms)
    n_value = len(value)
    span = wide // parts
    width = wide // len(sums)
    each = len(sums[0])

    def body(*refs):
        base_ref, state_ref, value_refs = refs[0], refs[1], refs[2 : 2 + n_value]
        sum_refs = refs[2 + n_value : 2 + n_value + n_sum]
        friction_ref, region_ref, partner_ref = refs[2 + n_value + n_sum : 5 + n_value + n_sum]
        outs = refs[5 + n_value + n_sum : -1]
        raw = refs[-1]
        for k in range(len(sums)):
            cols = pl.ds(k * width, width)
            total = sum_refs[k * each][...]
            for ref in sum_refs[k * each + 1 : (k + 1) * each]:
                total = total + ref[pl.ds(0, high), :]
            if last:
                total = sum_refs[-1][:, cols] + total
            elif part == 0:
                outs[2][:, cols] = total
            raw[:, cols] = base_ref[:, cols] + scale * total

        groups = high // 8

        def gather(cols):
            where = jnp.broadcast_to(partner_ref[:, cols], (8, LANES))
            lane = where % LANES
            block = where // LANES
            moved = [jnp.zeros((8, LANES), f32) for _ in range(groups)]
            for k in range(tiles):
                here = block == k
                for g in range(groups):
                    got = jnp.take_along_axis(
                        raw[pl.ds(g * 8, 8), pl.ds(k * LANES, LANES)], lane, axis=1, mode="promise_in_bounds"
                    )
                    moved[g] = jnp.where(here, got, moved[g])
            return moved

        def tiles_of(value_ref, begin, count):
            steps = count // LANES

            def place(j):
                return pl.ds(pl.multiple_of(part * span + begin + j * LANES, LANES), LANES)

            def tile(j, moved):
                cols = place(j)
                there = pl.ds(pl.multiple_of(j * LANES, LANES), LANES)
                into = pl.ds(pl.multiple_of(begin + j * LANES, LANES), LANES)
                later = gather(place(jnp.minimum(j + 1, steps - 1)))
                fric = jnp.broadcast_to(friction_ref[:, cols], (8, LANES))
                volume = jnp.broadcast_to(region_ref[:, cols], (8, LANES)) == 1
                for g in range(groups):
                    rows = pl.ds(g * 8, 8)
                    own = raw[rows, cols]
                    stress = own + coupling * (moved[g] - own)
                    new = newton(value_ref[rows, there], state_ref[rows, cols], stress, fric, volume)
                    outs[0][rows, into] = new
                    outs[1][rows, into] = stress if last else jnp.exp(new)
                return later

            lax.fori_loop(0, steps, tile, gather(place(0)))

        for k in range(n_value):
            tiles_of(value_refs[k], k * (span // n_value), span // n_value)

    full = jax.ShapeDtypeStruct((high, wide), f32)
    some = jax.ShapeDtypeStruct((high, span), f32)
    out_shape = [some, some] + ([full] if part == 0 and not last else [])
    return pl.pallas_call(
        body,
        grid=(1,),
        in_specs=[whole(a.shape) for a in (base, state, *value, *terms, friction, region, partner)],
        out_specs=[whole(a.shape) for a in out_shape],
        out_shape=out_shape,
        scratch_shapes=[pltpu.VMEM((high, wide), f32)],
        compiler_params=pltpu.CompilerParams(vmem_limit_bytes=24 << 20),
        cost_estimate=pl.CostEstimate(flops=200 * high * span, bytes_accessed=28 * high * wide, transcendentals=20 * high * span),
    )(base, state, *value, *terms, friction, region, partner)


def whole(shape):
    return pl.BlockSpec(shape, lambda *_: (0, 0), pipeline_mode=pl.Buffered(1))


def rates_times(halves, choice, kernel, part, parts, deps, tile=256):
    high, depth = halves[0][0][0].shape
    much = 4 * high
    rows = kernel.shape[0] // parts
    tile = min(tile, rows)
    steps = rows // tile
    flat = [
        pltpu.with_memory_space_constraint(ref, pltpu.HBM) for pairs in halves for pair in pairs for ref in pair
    ]

    def body(choice_ref, *refs):
        ins, kernel_ref = refs[:16], refs[16]
        own, across, other, stacked, landed, sem = refs[17 + len(deps) :]

        @pl.when(pl.program_id(0) == 0)
        def _():
            def fetch(k, ref):
                return pltpu.make_async_copy(ref, landed.at[k], sem.at[k])

            for k in range(8):

                @pl.when(choice_ref[0] == 0)
                def _():
                    fetch(k, ins[2 * k]).start()

                @pl.when(choice_ref[0] != 0)
                def _():
                    fetch(k, ins[2 * k + 1]).start()

            for k in range(8):
                fetch(k, ins[2 * k]).wait()
                cols = pl.ds((k // 4) * depth, depth)
                row = (k % 4) * high
                rates = landed[k]
                rough = rates.astype(bf16)
                stacked[pl.ds(row, high), cols] = rough
                stacked[pl.ds(much + row, high), cols] = (rates - rough.astype(f32)).astype(bf16)

        block = kernel_ref[...]
        upper = block.astype(bf16)
        lower = (block - upper.astype(f32)).astype(bf16)
        both = lax.dot_general(stacked[...], upper, NT, preferred_element_type=f32)
        rest = lax.dot_general(stacked[pl.ds(0, much), :], lower, NT, preferred_element_type=f32)
        total = both[:much] + both[much:] + rest
        own[...] = total[:high]
        across[...] = total[2 * high : 3 * high]
        other[pl.ds(0, high), :] = total[high : 2 * high]
        other[pl.ds(high, high), :] = total[3 * high :]

    one = pl.BlockSpec((high, tile), lambda i: (0, i))
    two = pl.BlockSpec((2 * high, tile), lambda i: (0, i))
    return pl.pallas_call(
        body,
        grid=(steps,),
        in_specs=[pl.BlockSpec(memory_space=pltpu.SMEM)]
        + [pl.BlockSpec(memory_space=pltpu.HBM)] * 16
        + [pl.BlockSpec((tile, 2 * depth), lambda i: (part * steps + i, 0))]
        + [CORNER] * len(deps),
        out_specs=[one, one, two],
        out_shape=[
            jax.ShapeDtypeStruct((high, rows), f32),
            jax.ShapeDtypeStruct((high, rows), f32),
            jax.ShapeDtypeStruct((2 * high, rows), f32),
        ],
        scratch_shapes=[
            pltpu.VMEM((2 * much, 2 * depth), bf16),
            pltpu.VMEM((8, high, depth), f32),
            pltpu.SemaphoreType.DMA((8,)),
        ],
        compiler_params=pltpu.CompilerParams(vmem_limit_bytes=24 << 20),
        cost_estimate=pl.CostEstimate(
            flops=24 * much * rows * depth, bytes_accessed=8 * rows * depth, transcendentals=0
        ),
    )(choice, *flat, pltpu.with_memory_space_constraint(kernel, pltpu.HBM), *deps)


OUTER = [(0, 1), (1, 0), (2, 3), (3, 2)]
INNER = [(0, 0), (1, 2), (2, 1), (3, 3)]
PLANE = ("col", "sub")
CORE = [(i, i ^ 1) for i in range(4)]
ACROSS = [(i, i ^ 2) for i in range(4)]


def where_sent():
    row = lax.axis_index("row")
    return (row == 1) | (row == 2), lax.axis_index("col") == row // 2


def spread_one(rates):
    return [lax.ppermute(rates, "row", OUTER), lax.ppermute(rates, "row", INNER)]


def spread_two(near):
    return [lax.ppermute(near[1], "row", OUTER), lax.ppermute(near[0], "row", INNER)]


def spread_three(two):
    return lax.ppermute(two[1], "row", OUTER)


def shift(first, second):
    beside = where_sent()[1]
    mine = jnp.where(beside, first, second)
    sent = jnp.where(beside, second, first)
    got = lax.ppermute(sent, PLANE, ACROSS)
    return [mine, lax.ppermute(mine, PLANE, CORE), got, lax.ppermute(got, PLANE, CORE)]


def spread(rates):
    middle = where_sent()[0]
    near = spread_one(rates)
    two = spread_two(near)
    far = spread_three(two)
    one = shift(rates, jnp.where(middle, near[1], two[0]))
    return list(zip(one, shift(near[0], jnp.where(middle, two[1], far))))


def first_block():
    row = lax.axis_index("row")
    beside = lax.axis_index("col") == row // 2
    near = jnp.where(beside, row, jnp.where(row < 2, 2, 1))
    return (near % 2 != lax.axis_index("sub")).astype(jnp.int32)[None]


def once(array, guard):
    return jnp.where(guard == guard, array, 0.0)


def spread_any(rates):
    blocks = lax.all_gather(rates, "row", axis=0)
    pieces = lax.all_to_all(blocks, ("col", "sub"), 0, 0)
    return [pieces[p] for p in range(pieces.shape[0])]


def sums_any(pieces, kernel):
    rates = jnp.concatenate(pieces, axis=0)
    partial = lax.dot_general(rates, kernel, NT, precision=lax.Precision.HIGH, preferred_element_type=f32)
    return [[lax.psum_scatter(partial, ("col", "sub"), scatter_dimension=0, tiled=True)]]


def solution(mesh):
    small = mesh.shape["row"] == 4 and mesh.shape["col"] == 2 and mesh.shape["sub"] == 2

    def plain(kernel, log_rate, state, base_stress, labels):
        sums = sums_any(spread_any(jnp.exp(log_rate)), kernel)
        value, rates, first = step_kernel(step_size, False, 0, 1, base_stress, [log_rate], state, sums, None, *labels)
        sums = sums_any(spread_any(rates), kernel)
        return tuple(step_kernel(0.5 * step_size, True, 0, 1, base_stress, [value], state, sums, first, *labels))

    def chunked(kernel, log_rate, state, base_stress, labels):
        wide = kernel.shape[1]
        choice = first_block()
        cuts = [slice(k * wide // 2, (k + 1) * wide // 2) for k in range(2)]

        def product(halves):
            sums = []
            for part in range(PARTS):
                deps = [sums[0][0], before] if sums else []
                own, across, other = rates_times(halves, choice, kernel, part, PARTS, deps)
                if sums:
                    stacked = other.reshape(2, *own.shape)
                    other = once(stacked, sums[0][2][None]).reshape(other.shape)
                swapped = lax.ppermute(other, PLANE, CORE)
                before = across + swapped[own.shape[0] :]
                sums.append([own, swapped, lax.ppermute(before, PLANE, ACROSS)])
            return sums

        rates = jnp.exp(log_rate)
        ready = spread(rates[:, cuts[0]])
        sums = product([ready, spread(rates[:, cuts[1]])])
        value, rates, first = step_kernel(
            step_size, False, 0, 2, base_stress, [log_rate[:, cuts[0]]], state, sums, None, *labels
        )
        ready = spread(rates)
        other_value, rates = step_kernel(
            step_size, False, 1, 2, base_stress, [log_rate[:, cuts[1]]], state, sums, None, *labels
        )
        sums = product([ready, spread(rates)])
        return tuple(
            step_kernel(
                0.5 * step_size, True, 0, 1, base_stress, [value, other_value], state, sums, first, *labels
            )
        )

    def per_device(kernel, log_rate, state, base_stress, friction, region, adjacency):
        partner = (adjacency - lax.axis_index("row") * kernel.shape[0])[None, :]
        labels = (friction[None, :], region[None, :], partner)
        return (chunked if small else plain)(kernel, log_rate, state, base_stress, labels)

    in_specs = (
        P("row", ("col", "sub")),
        P(("member", "col", "sub"), "row"),
        P(("member", "col", "sub"), "row"),
        P(("member", "col", "sub"), "row"),
        P("row"),
        P("row"),
        P("row"),
    )
    out_specs = (P(("member", "col", "sub"), "row"), P(("member", "col", "sub"), "row"))
    return jax.shard_map(per_device, mesh=mesh, in_specs=in_specs, out_specs=out_specs, check_vma=False)
```

```python
import jax
import jax.numpy as jnp
from jax import lax
from jax.experimental import pallas as pl
from jax.experimental.pallas import tpu as pltpu
from jax.sharding import PartitionSpec as P

NEWTON = 4
LANES = 128
PARTS = 2

coupling = 0.3
step_size = 0.5

f32 = jnp.float32
bf16 = jnp.bfloat16
NT = (((1,), (1,)), ((), ()))
CORNER = pl.BlockSpec((8, LANES), lambda *_: (0, 0))


def newton(value, state, stress, friction, volume):
    grow = jnp.exp(state)
    for turn in range(NEWTON):
        expo = jnp.exp(value)
        slipx = expo * grow
        square = 1.0 + slipx * slipx
        inverse = lax.rsqrt(square)
        fault_f = jnp.log(slipx + square * inverse)
        fault_d = slipx * inverse
        creep = grow * jnp.exp(value * (1.0 / 3.0))
        part_f = friction * jnp.where(volume, creep, fault_f)
        part_d = friction * jnp.where(volume, creep * (1.0 / 3.0), fault_d)
        value = value - jnp.clip((part_f + expo - stress) / (part_d + expo), -1.0, 1.0)
    return value


def step_kernel(scale, last, part, parts, base, value, state, sums, first, friction, region, partner):
    high, wide = base.shape
    tiles = wide // LANES
    terms = [a for group in sums for a in group] + ([first] if last else [])
    n_sum = len(terms)
    n_value = len(value)
    span = wide // parts
    width = wide // len(sums)
    each = len(sums[0])

    def body(*refs):
        base_ref, state_ref, value_refs = refs[0], refs[1], refs[2 : 2 + n_value]
        sum_refs = refs[2 + n_value : 2 + n_value + n_sum]
        friction_ref, region_ref, partner_ref = refs[2 + n_value + n_sum : 5 + n_value + n_sum]
        outs = refs[5 + n_value + n_sum : -1]
        raw = refs[-1]
        for k in range(len(sums)):
            cols = pl.ds(k * width, width)
            total = sum_refs[k * each][...]
            for ref in sum_refs[k * each + 1 : (k + 1) * each]:
                total = total + ref[pl.ds(0, high), :]
            if last:
                total = sum_refs[-1][:, cols] + total
            elif part == 0:
                outs[2][:, cols] = total
            raw[:, cols] = base_ref[:, cols] + scale * total

        groups = high // 8

        def gather(cols):
            where = jnp.broadcast_to(partner_ref[:, cols], (8, LANES))
            lane = where % LANES
            block = where // LANES
            moved = [jnp.zeros((8, LANES), f32) for _ in range(groups)]
            for k in range(tiles):
                here = block == k
                for g in range(groups):
                    got = jnp.take_along_axis(
                        raw[pl.ds(g * 8, 8), pl.ds(k * LANES, LANES)], lane, axis=1, mode="promise_in_bounds"
                    )
                    moved[g] = jnp.where(here, got, moved[g])
            return moved

        def tiles_of(value_ref, begin, count):
            steps = count // LANES

            def place(j):
                return pl.ds(pl.multiple_of(part * span + begin + j * LANES, LANES), LANES)

            def tile(j, moved):
                cols = place(j)
                there = pl.ds(pl.multiple_of(j * LANES, LANES), LANES)
                into = pl.ds(pl.multiple_of(begin + j * LANES, LANES), LANES)
                later = gather(place(jnp.minimum(j + 1, steps - 1)))
                fric = jnp.broadcast_to(friction_ref[:, cols], (8, LANES))
                volume = jnp.broadcast_to(region_ref[:, cols], (8, LANES)) == 1
                for g in range(groups):
                    rows = pl.ds(g * 8, 8)
                    own = raw[rows, cols]
                    stress = own + coupling * (moved[g] - own)
                    new = newton(value_ref[rows, there], state_ref[rows, cols], stress, fric, volume)
                    outs[0][rows, into] = new
                    outs[1][rows, into] = stress if last else jnp.exp(new)
                return later

            lax.fori_loop(0, steps, tile, gather(place(0)))

        for k in range(n_value):
            tiles_of(value_refs[k], k * (span // n_value), span // n_value)

    full = jax.ShapeDtypeStruct((high, wide), f32)
    some = jax.ShapeDtypeStruct((high, span), f32)
    out_shape = [some, some] + ([full] if part == 0 and not last else [])
    return pl.pallas_call(
        body,
        grid=(1,),
        in_specs=[whole(a.shape) for a in (base, state, *value, *terms, friction, region, partner)],
        out_specs=[whole(a.shape) for a in out_shape],
        out_shape=out_shape,
        scratch_shapes=[pltpu.VMEM((high, wide), f32)],
        compiler_params=pltpu.CompilerParams(vmem_limit_bytes=24 << 20),
        cost_estimate=pl.CostEstimate(flops=200 * high * span, bytes_accessed=28 * high * wide, transcendentals=20 * high * span),
    )(*(a if last else pltpu.with_memory_space_constraint(a, pltpu.HBM) for a in (base, state, *value)), *terms, friction, region, partner)


def whole(shape):
    return pl.BlockSpec(shape, lambda *_: (0, 0), pipeline_mode=pl.Buffered(1))


def rates_times(halves, choice, kernel, part, parts, deps, tile=256):
    high, depth = halves[0][0][0].shape
    much = 4 * high
    rows = kernel.shape[0] // parts
    tile = min(tile, rows)
    steps = rows // tile
    flat = [
        pltpu.with_memory_space_constraint(ref, pltpu.HBM) for pairs in halves for pair in pairs for ref in pair
    ]

    def body(choice_ref, *refs):
        ins, kernel_ref = refs[:16], refs[16]
        own, across, other, stacked, landed, sem = refs[17 + len(deps) :]

        @pl.when(pl.program_id(0) == 0)
        def _():
            def fetch(k, ref):
                return pltpu.make_async_copy(ref, landed.at[k], sem.at[k])

            for k in range(8):

                @pl.when(choice_ref[0] == 0)
                def _():
                    fetch(k, ins[2 * k]).start()

                @pl.when(choice_ref[0] != 0)
                def _():
                    fetch(k, ins[2 * k + 1]).start()

            for k in range(8):
                fetch(k, ins[2 * k]).wait()
                cols = pl.ds((k // 4) * depth, depth)
                row = (k % 4) * high
                rates = landed[k]
                rough = rates.astype(bf16)
                stacked[pl.ds(row, high), cols] = rough
                stacked[pl.ds(much + row, high), cols] = (rates - rough.astype(f32)).astype(bf16)

        block = kernel_ref[...]
        upper = block.astype(bf16)
        lower = (block - upper.astype(f32)).astype(bf16)
        both = lax.dot_general(stacked[...], upper, NT, preferred_element_type=f32)
        rest = lax.dot_general(stacked[pl.ds(0, much), :], lower, NT, preferred_element_type=f32)
        total = both[:much] + both[much:] + rest
        own[...] = total[:high]
        across[...] = total[2 * high : 3 * high]
        other[pl.ds(0, high), :] = total[high : 2 * high]
        other[pl.ds(high, high), :] = total[3 * high :]

    one = pl.BlockSpec((high, tile), lambda i: (0, i))
    two = pl.BlockSpec((2 * high, tile), lambda i: (0, i))
    return pl.pallas_call(
        body,
        grid=(steps,),
        in_specs=[pl.BlockSpec(memory_space=pltpu.SMEM)]
        + [pl.BlockSpec(memory_space=pltpu.HBM)] * 16
        + [pl.BlockSpec((tile, 2 * depth), lambda i: (part * steps + i, 0))]
        + [CORNER] * len(deps),
        out_specs=[one, one, two],
        out_shape=[
            jax.ShapeDtypeStruct((high, rows), f32),
            jax.ShapeDtypeStruct((high, rows), f32),
            jax.ShapeDtypeStruct((2 * high, rows), f32),
        ],
        scratch_shapes=[
            pltpu.VMEM((2 * much, 2 * depth), bf16),
            pltpu.VMEM((8, high, depth), f32),
            pltpu.SemaphoreType.DMA((8,)),
        ],
        compiler_params=pltpu.CompilerParams(vmem_limit_bytes=24 << 20),
        cost_estimate=pl.CostEstimate(
            flops=24 * much * rows * depth, bytes_accessed=8 * rows * depth, transcendentals=0
        ),
    )(choice, *flat, pltpu.with_memory_space_constraint(kernel, pltpu.HBM), *deps)


OUTER = [(0, 1), (1, 0), (2, 3), (3, 2)]
INNER = [(0, 0), (1, 2), (2, 1), (3, 3)]
PLANE = ("col", "sub")
CORE = [(i, i ^ 1) for i in range(4)]
ACROSS = [(i, i ^ 2) for i in range(4)]


def where_sent():
    row = lax.axis_index("row")
    return (row == 1) | (row == 2), lax.axis_index("col") == row // 2


def spread_one(rates):
    return [lax.ppermute(rates, "row", OUTER), lax.ppermute(rates, "row", INNER)]


def spread_two(near):
    return [lax.ppermute(near[1], "row", OUTER), lax.ppermute(near[0], "row", INNER)]


def spread_three(two):
    return lax.ppermute(two[1], "row", OUTER)


def shift(first, second, guard=None):
    beside = where_sent()[1]
    mine = jnp.where(beside, first, second)
    sent = jnp.where(beside, second, first)
    if guard is not None:
        sent = once(sent, guard)
    got = lax.ppermute(sent, PLANE, ACROSS)
    return [mine, lax.ppermute(mine, PLANE, CORE), got, lax.ppermute(got, PLANE, CORE)]


def along(rates, guard=None):
    near = spread_one(rates)
    two = spread_two(near)
    if guard is not None:
        return rates, near, two, spread_three([two[0], once(two[1], guard)])
    return rates, near, two, spread_three(two)


def spread(halves, ordered):
    middle = where_sent()[0]
    one = [shift(rates, jnp.where(middle, near[1], two[0])) for rates, near, two, far in halves]
    guard = one[1][2] if ordered else None
    pairs = []
    for k, (rates, near, two, far) in enumerate(halves):
        last = shift(near[0], jnp.where(middle, two[1], far), guard)
        pairs.append(list(zip(one[k], last)))
        guard = last[2] if ordered else None
    return pairs


def first_block():
    row = lax.axis_index("row")
    beside = lax.axis_index("col") == row // 2
    near = jnp.where(beside, row, jnp.where(row < 2, 2, 1))
    return (near % 2 != lax.axis_index("sub")).astype(jnp.int32)[None]


def once(array, guard):
    return jnp.where(guard == guard, array, 0.0)


def spread_any(rates):
    blocks = lax.all_gather(rates, "row", axis=0)
    pieces = lax.all_to_all(blocks, ("col", "sub"), 0, 0)
    return [pieces[p] for p in range(pieces.shape[0])]


def sums_any(pieces, kernel):
    rates = jnp.concatenate(pieces, axis=0)
    partial = lax.dot_general(rates, kernel, NT, precision=lax.Precision.HIGH, preferred_element_type=f32)
    return [[lax.psum_scatter(partial, ("col", "sub"), scatter_dimension=0, tiled=True)]]


def solution(mesh):
    small = mesh.shape["row"] == 4 and mesh.shape["col"] == 2 and mesh.shape["sub"] == 2

    def plain(kernel, log_rate, state, base_stress, labels):
        sums = sums_any(spread_any(jnp.exp(log_rate)), kernel)
        value, rates, first = step_kernel(step_size, False, 0, 1, base_stress, [log_rate], state, sums, None, *labels)
        sums = sums_any(spread_any(rates), kernel)
        return tuple(step_kernel(0.5 * step_size, True, 0, 1, base_stress, [value], state, sums, first, *labels))

    def chunked(kernel, log_rate, state, base_stress, labels):
        wide = kernel.shape[1]
        choice = first_block()
        cuts = [slice(k * wide // 2, (k + 1) * wide // 2) for k in range(2)]

        def product(halves):
            sums = []
            for part in range(PARTS):
                deps = [sums[0][0], before] if sums else []
                own, across, other = rates_times(halves, choice, kernel, part, PARTS, deps)
                if sums:
                    stacked = other.reshape(2, *own.shape)
                    other = once(stacked, sums[0][2][None]).reshape(other.shape)
                swapped = lax.ppermute(other, PLANE, CORE)
                before = across + swapped[own.shape[0] :]
                sums.append([own, swapped, lax.ppermute(before, PLANE, ACROSS)])
            return sums

        rates = jnp.exp(log_rate)
        sums = product(spread([along(rates[:, cut]) for cut in cuts], False))
        value, rates, first = step_kernel(
            step_size, False, 0, 2, base_stress, [log_rate[:, cuts[0]]], state, sums, None, *labels
        )
        ready = along(rates)
        other_value, rates = step_kernel(
            step_size, False, 1, 2, base_stress, [log_rate[:, cuts[1]]], state, sums, None, *labels
        )
        sums = product(spread([ready, along(rates)], False))
        return tuple(
            step_kernel(
                0.5 * step_size, True, 0, 1, base_stress, [value, other_value], state, sums, first, *labels
            )
        )

    def per_device(kernel, log_rate, state, base_stress, friction, region, adjacency):
        partner = (adjacency - lax.axis_index("row") * kernel.shape[0])[None, :]
        labels = (friction[None, :], region[None, :], partner)
        return (chunked if small else plain)(kernel, log_rate, state, base_stress, labels)

    in_specs = (
        P("row", ("col", "sub")),
        P(("member", "col", "sub"), "row"),
        P(("member", "col", "sub"), "row"),
        P(("member", "col", "sub"), "row"),
        P("row"),
        P("row"),
        P("row"),
    )
    out_specs = (P(("member", "col", "sub"), "row"), P(("member", "col", "sub"), "row"))
    return jax.shard_map(per_device, mesh=mesh, in_specs=in_specs, out_specs=out_specs, check_vma=False)
```

```python
import jax
import jax.numpy as jnp
from jax import lax
from jax.experimental import pallas as pl
from jax.experimental.pallas import tpu as pltpu
from jax.sharding import PartitionSpec as P

NEWTON = 4
LANES = 128
PARTS = 2

coupling = 0.3
step_size = 0.5

f32 = jnp.float32
bf16 = jnp.bfloat16
NT = (((1,), (1,)), ((), ()))
CORNER = pl.BlockSpec((8, LANES), lambda *_: (0, 0))


def newton(value, state, stress, friction, volume):
    grow = jnp.exp(state)
    for turn in range(NEWTON):
        expo = jnp.exp(value)
        slipx = expo * grow
        square = 1.0 + slipx * slipx
        inverse = lax.rsqrt(square)
        fault_f = jnp.log(slipx + square * inverse)
        fault_d = slipx * inverse
        creep = grow * jnp.exp(value * (1.0 / 3.0))
        part_f = friction * jnp.where(volume, creep, fault_f)
        part_d = friction * jnp.where(volume, creep * (1.0 / 3.0), fault_d)
        value = value - jnp.clip((part_f + expo - stress) / (part_d + expo), -1.0, 1.0)
    return value


def step_kernel(scale, last, part, parts, base, value, state, sums, first, friction, region, partner):
    high, wide = base.shape
    tiles = wide // LANES
    terms = [a for group in sums for a in group] + ([first] if last else [])
    n_sum = len(terms)
    n_value = len(value)
    span = wide // parts
    width = wide // len(sums)
    each = len(sums[0])

    def body(*refs):
        base_ref, state_ref, value_refs = refs[0], refs[1], refs[2 : 2 + n_value]
        sum_refs = refs[2 + n_value : 2 + n_value + n_sum]
        friction_ref, region_ref, partner_ref = refs[2 + n_value + n_sum : 5 + n_value + n_sum]
        outs = refs[5 + n_value + n_sum : -1]
        raw = refs[-1]
        for k in range(len(sums)):
            cols = pl.ds(k * width, width)
            total = sum_refs[k * each][...]
            for ref in sum_refs[k * each + 1 : (k + 1) * each]:
                total = total + ref[pl.ds(0, high), :]
            if last:
                total = sum_refs[-1][:, cols] + total
            elif part == 0:
                outs[2][:, cols] = total
            raw[:, cols] = base_ref[:, cols] + scale * total

        groups = high // 8

        def gather(cols):
            where = jnp.broadcast_to(partner_ref[:, cols], (8, LANES))
            lane = where % LANES
            block = where // LANES
            moved = [jnp.zeros((8, LANES), f32) for _ in range(groups)]
            for k in range(tiles):
                here = block == k
                for g in range(groups):
                    got = jnp.take_along_axis(
                        raw[pl.ds(g * 8, 8), pl.ds(k * LANES, LANES)], lane, axis=1, mode="promise_in_bounds"
                    )
                    moved[g] = jnp.where(here, got, moved[g])
            return moved

        def tiles_of(value_ref, begin, count):
            steps = count // LANES

            def place(j):
                return pl.ds(pl.multiple_of(part * span + begin + j * LANES, LANES), LANES)

            def tile(j, moved):
                cols = place(j)
                there = pl.ds(pl.multiple_of(j * LANES, LANES), LANES)
                into = pl.ds(pl.multiple_of(begin + j * LANES, LANES), LANES)
                later = gather(place(jnp.minimum(j + 1, steps - 1)))
                fric = jnp.broadcast_to(friction_ref[:, cols], (8, LANES))
                volume = jnp.broadcast_to(region_ref[:, cols], (8, LANES)) == 1
                for g in range(groups):
                    rows = pl.ds(g * 8, 8)
                    own = raw[rows, cols]
                    stress = own + coupling * (moved[g] - own)
                    new = newton(value_ref[rows, there], state_ref[rows, into], stress, fric, volume)
                    outs[0][rows, into] = new
                    outs[1][rows, into] = stress if last else jnp.exp(new)
                return later

            lax.fori_loop(0, steps, tile, gather(place(0)))

        for k in range(n_value):
            tiles_of(value_refs[k], k * (span // n_value), span // n_value)

    full = jax.ShapeDtypeStruct((high, wide), f32)
    some = jax.ShapeDtypeStruct((high, span), f32)
    out_shape = [some, some] + ([full] if part == 0 and not last else [])
    return pl.pallas_call(
        body,
        grid=(1,),
        in_specs=[
            whole(base.shape),
            pl.BlockSpec((high, span), lambda *_: (0, part), pipeline_mode=pl.Buffered(1)),
            *(whole((high, a.shape[1])) for a in (*value, *terms)),
            *(whole(a.shape) for a in (friction, region, partner)),
        ],
        out_specs=[whole(a.shape) for a in out_shape],
        out_shape=out_shape,
        scratch_shapes=[pltpu.VMEM((high, wide), f32)],
        compiler_params=pltpu.CompilerParams(vmem_limit_bytes=24 << 20),
        cost_estimate=pl.CostEstimate(flops=200 * high * span, bytes_accessed=28 * high * wide, transcendentals=20 * high * span),
    )(*(a if last else pltpu.with_memory_space_constraint(a, pltpu.HBM) for a in (base, state, *value)), *terms, friction, region, partner)


def whole(shape):
    return pl.BlockSpec(shape, lambda *_: (0, 0), pipeline_mode=pl.Buffered(1))


def rates_times(halves, choice, kernel, part, parts, deps, tile=256):
    high, depth = halves[0][0][0].shape
    much = 4 * high
    rows = kernel.shape[0] // parts
    tile = min(tile, rows)
    steps = rows // tile
    flat = [
        pltpu.with_memory_space_constraint(ref, pltpu.HBM) for pairs in halves for pair in pairs for ref in pair
    ]

    def body(choice_ref, *refs):
        ins, kernel_ref = refs[:16], refs[16]
        own, across, other, stacked, landed, sem = refs[17 + len(deps) :]

        @pl.when(pl.program_id(0) == 0)
        def _():
            def fetch(k, ref):
                return pltpu.make_async_copy(ref, landed.at[k], sem.at[k])

            for k in range(8):

                @pl.when(choice_ref[0] == 0)
                def _():
                    fetch(k, ins[2 * k]).start()

                @pl.when(choice_ref[0] != 0)
                def _():
                    fetch(k, ins[2 * k + 1]).start()

            for k in range(8):
                fetch(k, ins[2 * k]).wait()
                cols = pl.ds((k // 4) * depth, depth)
                row = (k % 4) * high
                rates = landed[k]
                rough = rates.astype(bf16)
                stacked[pl.ds(row, high), cols] = rough
                stacked[pl.ds(much + row, high), cols] = (rates - rough.astype(f32)).astype(bf16)

        block = kernel_ref[...]
        upper = block.astype(bf16)
        lower = (block - upper.astype(f32)).astype(bf16)
        both = lax.dot_general(stacked[...], upper, NT, preferred_element_type=f32)
        rest = lax.dot_general(stacked[pl.ds(0, much), :], lower, NT, preferred_element_type=f32)
        total = both[:much] + both[much:] + rest
        own[...] = total[:high]
        across[...] = total[2 * high : 3 * high]
        other[pl.ds(0, high), :] = total[high : 2 * high]
        other[pl.ds(high, high), :] = total[3 * high :]

    one = pl.BlockSpec((high, tile), lambda i: (0, i))
    two = pl.BlockSpec((2 * high, tile), lambda i: (0, i))
    return pl.pallas_call(
        body,
        grid=(steps,),
        in_specs=[pl.BlockSpec(memory_space=pltpu.SMEM)]
        + [pl.BlockSpec(memory_space=pltpu.HBM)] * 16
        + [pl.BlockSpec((tile, 2 * depth), lambda i: (part * steps + i, 0))]
        + [CORNER] * len(deps),
        out_specs=[one, one, two],
        out_shape=[
            jax.ShapeDtypeStruct((high, rows), f32),
            jax.ShapeDtypeStruct((high, rows), f32),
            jax.ShapeDtypeStruct((2 * high, rows), f32),
        ],
        scratch_shapes=[
            pltpu.VMEM((2 * much, 2 * depth), bf16),
            pltpu.VMEM((8, high, depth), f32),
            pltpu.SemaphoreType.DMA((8,)),
        ],
        compiler_params=pltpu.CompilerParams(vmem_limit_bytes=24 << 20),
        cost_estimate=pl.CostEstimate(
            flops=24 * much * rows * depth, bytes_accessed=8 * rows * depth, transcendentals=0
        ),
    )(choice, *flat, pltpu.with_memory_space_constraint(kernel, pltpu.HBM), *deps)


OUTER = [(0, 1), (1, 0), (2, 3), (3, 2)]
INNER = [(0, 0), (1, 2), (2, 1), (3, 3)]
PLANE = ("col", "sub")
CORE = [(i, i ^ 1) for i in range(4)]
ACROSS = [(i, i ^ 2) for i in range(4)]


def where_sent():
    row = lax.axis_index("row")
    return (row == 1) | (row == 2), lax.axis_index("col") == row // 2


def spread_one(rates):
    return [lax.ppermute(rates, "row", OUTER), lax.ppermute(rates, "row", INNER)]


def spread_two(near):
    return [lax.ppermute(near[1], "row", OUTER), lax.ppermute(near[0], "row", INNER)]


def spread_three(two):
    return lax.ppermute(two[1], "row", OUTER)


def shift(first, second, guard=None):
    beside = where_sent()[1]
    mine = jnp.where(beside, first, second)
    sent = jnp.where(beside, second, first)
    if guard is not None:
        sent = once(sent, guard)
    got = lax.ppermute(sent, PLANE, ACROSS)
    return [mine, lax.ppermute(mine, PLANE, CORE), got, lax.ppermute(got, PLANE, CORE)]


def along(rates, guard=None):
    near = spread_one(rates)
    two = spread_two(near)
    if guard is not None:
        return rates, near, two, spread_three([two[0], once(two[1], guard)])
    return rates, near, two, spread_three(two)


def spread(halves, ordered):
    middle = where_sent()[0]
    one = [shift(rates, jnp.where(middle, near[1], two[0])) for rates, near, two, far in halves]
    guard = one[1][2] if ordered else None
    pairs = []
    for k, (rates, near, two, far) in enumerate(halves):
        last = shift(near[0], jnp.where(middle, two[1], far), guard)
        pairs.append(list(zip(one[k], last)))
        guard = last[2] if ordered else None
    return pairs


def first_block():
    row = lax.axis_index("row")
    beside = lax.axis_index("col") == row // 2
    near = jnp.where(beside, row, jnp.where(row < 2, 2, 1))
    return (near % 2 != lax.axis_index("sub")).astype(jnp.int32)[None]


def once(array, guard):
    return jnp.where(guard == guard, array, 0.0)


def spread_any(rates):
    blocks = lax.all_gather(rates, "row", axis=0)
    pieces = lax.all_to_all(blocks, ("col", "sub"), 0, 0)
    return [pieces[p] for p in range(pieces.shape[0])]


def sums_any(pieces, kernel):
    rates = jnp.concatenate(pieces, axis=0)
    partial = lax.dot_general(rates, kernel, NT, precision=lax.Precision.HIGH, preferred_element_type=f32)
    return [[lax.psum_scatter(partial, ("col", "sub"), scatter_dimension=0, tiled=True)]]


def solution(mesh):
    small = mesh.shape["row"] == 4 and mesh.shape["col"] == 2 and mesh.shape["sub"] == 2

    def plain(kernel, log_rate, state, base_stress, labels):
        sums = sums_any(spread_any(jnp.exp(log_rate)), kernel)
        value, rates, first = step_kernel(step_size, False, 0, 1, base_stress, [log_rate], state, sums, None, *labels)
        sums = sums_any(spread_any(rates), kernel)
        return tuple(step_kernel(0.5 * step_size, True, 0, 1, base_stress, [value], state, sums, first, *labels))

    def chunked(kernel, log_rate, state, base_stress, labels):
        wide = kernel.shape[1]
        choice = first_block()
        cuts = [slice(k * wide // 2, (k + 1) * wide // 2) for k in range(2)]

        def product(halves):
            sums = []
            for part in range(PARTS):
                deps = [sums[0][0], before] if sums else []
                own, across, other = rates_times(halves, choice, kernel, part, PARTS, deps)
                if sums:
                    stacked = other.reshape(2, *own.shape)
                    other = once(stacked, sums[0][2][None]).reshape(other.shape)
                swapped = lax.ppermute(other, PLANE, CORE)
                before = across + swapped[own.shape[0] :]
                sums.append([own, swapped, lax.ppermute(before, PLANE, ACROSS)])
            return sums

        rates = jnp.exp(log_rate)
        sums = product(spread([along(rates[:, cut]) for cut in cuts], False))
        value, rates, first = step_kernel(
            step_size, False, 0, 2, base_stress, [log_rate[:, cuts[0]]], state, sums, None, *labels
        )
        ready = along(rates)
        other_value, rates = step_kernel(
            step_size, False, 1, 2, base_stress, [log_rate[:, cuts[1]]], state, sums, None, *labels
        )
        sums = product(spread([ready, along(rates)], False))
        return tuple(
            step_kernel(
                0.5 * step_size, True, 0, 1, base_stress, [value, other_value], state, sums, first, *labels
            )
        )

    def per_device(kernel, log_rate, state, base_stress, friction, region, adjacency):
        partner = (adjacency - lax.axis_index("row") * kernel.shape[0])[None, :]
        labels = (friction[None, :], region[None, :], partner)
        return (chunked if small else plain)(kernel, log_rate, state, base_stress, labels)

    in_specs = (
        P("row", ("col", "sub")),
        P(("member", "col", "sub"), "row"),
        P(("member", "col", "sub"), "row"),
        P(("member", "col", "sub"), "row"),
        P("row"),
        P("row"),
        P("row"),
    )
    out_specs = (P(("member", "col", "sub"), "row"), P(("member", "col", "sub"), "row"))
    return jax.shard_map(per_device, mesh=mesh, in_specs=in_specs, out_specs=out_specs, check_vma=False)
```

```python
import jax
import jax.numpy as jnp
from jax import lax
from jax.experimental import pallas as pl
from jax.experimental.pallas import tpu as pltpu
from jax.sharding import PartitionSpec as P

NEWTON = 4
LANES = 128
PARTS = 2

coupling = 0.3
step_size = 0.5

f32 = jnp.float32
bf16 = jnp.bfloat16
NT = (((1,), (1,)), ((), ()))
CORNER = pl.BlockSpec((8, LANES), lambda *_: (0, 0))


def newton(value, state, stress, friction, volume):
    grow = jnp.exp(state)
    for turn in range(NEWTON):
        expo = jnp.exp(value)
        slipx = expo * grow
        square = 1.0 + slipx * slipx
        inverse = lax.rsqrt(square)
        fault_f = jnp.log(slipx + square * inverse)
        fault_d = slipx * inverse
        creep = grow * jnp.exp(value * (1.0 / 3.0))
        part_f = friction * jnp.where(volume, creep, fault_f)
        part_d = friction * jnp.where(volume, creep * (1.0 / 3.0), fault_d)
        value = value - jnp.clip((part_f + expo - stress) / (part_d + expo), -1.0, 1.0)
    return value


def step_kernel(scale, last, part, parts, base, value, state, sums, first, friction, region, partner):
    high, wide = base.shape
    tiles = wide // LANES
    terms = [a for group in sums for a in group] + ([first] if last else [])
    n_sum = len(terms)
    n_value = len(value)
    span = wide // parts
    width = wide // len(sums)
    each = len(sums[0])

    def body(*refs):
        base_ref, state_ref, value_refs = refs[0], refs[1], refs[2 : 2 + n_value]
        sum_refs = refs[2 + n_value : 2 + n_value + n_sum]
        friction_ref, region_ref, partner_ref = refs[2 + n_value + n_sum : 5 + n_value + n_sum]
        outs = refs[5 + n_value + n_sum : -1]
        raw = refs[-1]
        for k in range(len(sums)):
            cols = pl.ds(k * width, width)
            total = sum_refs[k * each][...]
            for ref in sum_refs[k * each + 1 : (k + 1) * each]:
                total = total + ref[pl.ds(0, high), :]
            if last:
                total = sum_refs[-1][:, cols] + total
            elif part == 0:
                outs[2][:, cols] = total
            raw[:, cols] = base_ref[:, cols] + scale * total

        groups = high // 8

        def gather(cols):
            where = jnp.broadcast_to(partner_ref[:, cols], (8, LANES))
            lane = where % LANES
            block = where // LANES
            moved = [jnp.zeros((8, LANES), f32) for _ in range(groups)]
            for k in range(tiles):
                here = block == k
                for g in range(groups):
                    got = jnp.take_along_axis(
                        raw[pl.ds(g * 8, 8), pl.ds(k * LANES, LANES)], lane, axis=1, mode="promise_in_bounds"
                    )
                    moved[g] = jnp.where(here, got, moved[g])
            return moved

        def tiles_of(value_ref, begin, count):
            steps = count // LANES

            def place(j):
                return pl.ds(pl.multiple_of(part * span + begin + j * LANES, LANES), LANES)

            def tile(j, moved):
                cols = place(j)
                there = pl.ds(pl.multiple_of(j * LANES, LANES), LANES)
                into = pl.ds(pl.multiple_of(begin + j * LANES, LANES), LANES)
                later = gather(place(jnp.minimum(j + 1, steps - 1)))
                fric = jnp.broadcast_to(friction_ref[:, cols], (8, LANES))
                volume = jnp.broadcast_to(region_ref[:, cols], (8, LANES)) == 1
                for g in range(groups):
                    rows = pl.ds(g * 8, 8)
                    own = raw[rows, cols]
                    stress = own + coupling * (moved[g] - own)
                    new = newton(value_ref[rows, there], state_ref[rows, into], stress, fric, volume)
                    outs[0][rows, into] = new
                    outs[1][rows, into] = stress if last else jnp.exp(new)
                return later

            lax.fori_loop(0, steps, tile, gather(place(0)))

        for k in range(n_value):
            tiles_of(value_refs[k], k * (span // n_value), span // n_value)

    full = jax.ShapeDtypeStruct((high, wide), f32)
    some = jax.ShapeDtypeStruct((high, span), f32)
    out_shape = [some, some] + ([full] if part == 0 and not last else [])
    return pl.pallas_call(
        body,
        grid=(1,),
        in_specs=[
            whole(base.shape),
            pl.BlockSpec((high, span), lambda *_: (0, part), pipeline_mode=pl.Buffered(1)),
            *(whole((high, a.shape[1])) for a in (*value, *terms)),
            *(whole(a.shape) for a in (friction, region, partner)),
        ],
        out_specs=[whole(a.shape) for a in out_shape],
        out_shape=out_shape,
        scratch_shapes=[pltpu.VMEM((high, wide), f32)],
        compiler_params=pltpu.CompilerParams(vmem_limit_bytes=24 << 20),
        cost_estimate=pl.CostEstimate(flops=200 * high * span, bytes_accessed=28 * high * wide, transcendentals=20 * high * span),
    )(*(a if last else pltpu.with_memory_space_constraint(a, pltpu.HBM) for a in (base, state, *value)), *terms, friction, region, partner)


def whole(shape):
    return pl.BlockSpec(shape, lambda *_: (0, 0), pipeline_mode=pl.Buffered(1))


def rates_times(halves, choice, kernel, part, parts, deps, tile=256):
    high, depth = halves[0][0][0].shape
    much = 4 * high
    rows = kernel.shape[0] // parts
    tile = min(tile, rows)
    steps = rows // tile
    flat = [
        pltpu.with_memory_space_constraint(ref, pltpu.HBM) for pairs in halves for pair in pairs for ref in pair
    ]

    def body(choice_ref, *refs):
        ins, kernel_ref = refs[:16], refs[16]
        own, across, other, stacked, landed, sem = refs[17 + len(deps) :]

        @pl.when(pl.program_id(0) == 0)
        def _():
            def fetch(k, ref):
                return pltpu.make_async_copy(ref, landed.at[k], sem.at[k])

            for k in range(8):

                @pl.when(choice_ref[0] == 0)
                def _():
                    fetch(k, ins[2 * k]).start()

                @pl.when(choice_ref[0] != 0)
                def _():
                    fetch(k, ins[2 * k + 1]).start()

            for k in range(8):
                fetch(k, ins[2 * k]).wait()
                cols = pl.ds((k // 4) * depth, depth)
                row = (k % 4) * high
                rates = landed[k]
                rough = rates.astype(bf16)
                stacked[pl.ds(row, high), cols] = rough
                stacked[pl.ds(much + row, high), cols] = (rates - rough.astype(f32)).astype(bf16)

        block = kernel_ref[...]
        upper = block.astype(bf16)
        lower = (block - upper.astype(f32)).astype(bf16)
        both = lax.dot_general(stacked[...], upper, NT, preferred_element_type=f32)
        rest = lax.dot_general(stacked[pl.ds(0, much), :], lower, NT, preferred_element_type=f32)
        total = both[:much] + both[much:] + rest
        own[...] = total[:high]
        across[...] = total[2 * high : 3 * high]
        other[pl.ds(0, high), :] = total[high : 2 * high]
        other[pl.ds(high, high), :] = total[3 * high :]

    one = pl.BlockSpec((high, tile), lambda i: (0, i))
    two = pl.BlockSpec((2 * high, tile), lambda i: (0, i))
    return pl.pallas_call(
        body,
        grid=(steps,),
        in_specs=[pl.BlockSpec(memory_space=pltpu.SMEM)]
        + [pl.BlockSpec(memory_space=pltpu.HBM)] * 16
        + [pl.BlockSpec((tile, 2 * depth), lambda i: (part * steps + i, 0))]
        + [CORNER] * len(deps),
        out_specs=[one, one, two],
        out_shape=[
            jax.ShapeDtypeStruct((high, rows), f32),
            jax.ShapeDtypeStruct((high, rows), f32),
            jax.ShapeDtypeStruct((2 * high, rows), f32),
        ],
        scratch_shapes=[
            pltpu.VMEM((2 * much, 2 * depth), bf16),
            pltpu.VMEM((8, high, depth), f32),
            pltpu.SemaphoreType.DMA((8,)),
        ],
        compiler_params=pltpu.CompilerParams(vmem_limit_bytes=24 << 20),
        cost_estimate=pl.CostEstimate(
            flops=24 * much * rows * depth, bytes_accessed=8 * rows * depth, transcendentals=0
        ),
    )(choice, *flat, pltpu.with_memory_space_constraint(kernel, pltpu.HBM), *deps)


OUTER = [(0, 1), (1, 0), (2, 3), (3, 2)]
INNER = [(0, 0), (1, 2), (2, 1), (3, 3)]
PLANE = ("col", "sub")
CORE = [(i, i ^ 1) for i in range(4)]
ACROSS = [(i, i ^ 2) for i in range(4)]


def where_sent():
    row = lax.axis_index("row")
    return (row == 1) | (row == 2), lax.axis_index("col") == row // 2


def spread_one(rates):
    return [lax.ppermute(rates, "row", OUTER), lax.ppermute(rates, "row", INNER)]


def spread_two(near):
    return [lax.ppermute(near[1], "row", OUTER), lax.ppermute(near[0], "row", INNER)]


def spread_three(two):
    return lax.ppermute(two[1], "row", OUTER)


def shift(first, second, guard=None):
    beside = where_sent()[1]
    mine = jnp.where(beside, first, second)
    sent = jnp.where(beside, second, first)
    if guard is not None:
        sent = once(sent, guard)
    got = lax.ppermute(sent, PLANE, ACROSS)
    return [mine, lax.ppermute(mine, PLANE, CORE), got, lax.ppermute(got, PLANE, CORE)]


def along(rates, guard=None):
    near = spread_one(rates)
    two = spread_two(near)
    if guard is not None:
        return rates, near, two, spread_three([two[0], once(two[1], guard)])
    return rates, near, two, spread_three(two)


def spread(halves, ordered):
    middle = where_sent()[0]
    one = [shift(rates, jnp.where(middle, near[1], two[0])) for rates, near, two, far in halves]
    guard = one[1][2] if ordered else None
    pairs = []
    for k, (rates, near, two, far) in enumerate(halves):
        last = shift(near[0], jnp.where(middle, two[1], far), guard)
        pairs.append(list(zip(one[k], last)))
        guard = last[2] if ordered else None
    return pairs


def first_block():
    row = lax.axis_index("row")
    beside = lax.axis_index("col") == row // 2
    near = jnp.where(beside, row, jnp.where(row < 2, 2, 1))
    return (near % 2 != lax.axis_index("sub")).astype(jnp.int32)[None]


def once(array, guard):
    return jnp.where(guard == guard, array, 0.0)


def spread_any(rates):
    blocks = lax.all_gather(rates, "row", axis=0)
    pieces = lax.all_to_all(blocks, ("col", "sub"), 0, 0)
    return [pieces[p] for p in range(pieces.shape[0])]


def sums_any(pieces, kernel):
    rates = jnp.concatenate(pieces, axis=0)
    partial = lax.dot_general(rates, kernel, NT, precision=lax.Precision.HIGH, preferred_element_type=f32)
    return [[lax.psum_scatter(partial, ("col", "sub"), scatter_dimension=0, tiled=True)]]


def solution(mesh):
    small = mesh.shape["row"] == 4 and mesh.shape["col"] == 2 and mesh.shape["sub"] == 2

    def plain(kernel, log_rate, state, base_stress, labels):
        sums = sums_any(spread_any(jnp.exp(log_rate)), kernel)
        value, rates, first = step_kernel(step_size, False, 0, 1, base_stress, [log_rate], state, sums, None, *labels)
        sums = sums_any(spread_any(rates), kernel)
        return tuple(step_kernel(0.5 * step_size, True, 0, 1, base_stress, [value], state, sums, first, *labels))

    def chunked(kernel, log_rate, state, base_stress, labels):
        wide = kernel.shape[1]
        choice = first_block()
        cuts = [slice(k * wide // 2, (k + 1) * wide // 2) for k in range(2)]

        def product(halves):
            sums = []
            for part in range(PARTS):
                deps = [sums[0][0], before] if sums else []
                own, across, other = rates_times(halves, choice, kernel, part, PARTS, deps)
                if sums:
                    stacked = other.reshape(2, *own.shape)
                    other = once(stacked, sums[0][2][None]).reshape(other.shape)
                swapped = lax.ppermute(other, PLANE, CORE)
                before = across + swapped[own.shape[0] :]
                sums.append([own, swapped, lax.ppermute(before, PLANE, ACROSS)])
            return sums

        sums = product(spread([along(jnp.exp(log_rate[:, cut])) for cut in cuts], False))
        value, rates, first = step_kernel(
            step_size, False, 0, 2, base_stress, [log_rate[:, cuts[0]]], state, sums, None, *labels
        )
        ready = along(rates)
        other_value, rates = step_kernel(
            step_size, False, 1, 2, base_stress, [log_rate[:, cuts[1]]], state, sums, None, *labels
        )
        sums = product(spread([ready, along(rates)], False))
        return tuple(
            step_kernel(
                0.5 * step_size, True, 0, 1, base_stress, [value, other_value], state, sums, first, *labels
            )
        )

    def per_device(kernel, log_rate, state, base_stress, friction, region, adjacency):
        partner = (adjacency - lax.axis_index("row") * kernel.shape[0])[None, :]
        labels = (friction[None, :], region[None, :], partner)
        return (chunked if small else plain)(kernel, log_rate, state, base_stress, labels)

    in_specs = (
        P("row", ("col", "sub")),
        P(("member", "col", "sub"), "row"),
        P(("member", "col", "sub"), "row"),
        P(("member", "col", "sub"), "row"),
        P("row"),
        P("row"),
        P("row"),
    )
    out_specs = (P(("member", "col", "sub"), "row"), P(("member", "col", "sub"), "row"))
    return jax.shard_map(per_device, mesh=mesh, in_specs=in_specs, out_specs=out_specs, check_vma=False)
```
